512 devices in a mesh: seq: 32 (over x, z), ep: 16 (over y, core).
Axes of the slice: x: 4, y: 8, z: 8, core: 2. Of those that a mesh axis runs over, the one named last changes fastest.
Arguments:
- queries: bfloat16 [16, 4096, 2048], P('ep', 'seq'), may hold values from -6 to 6
- key_rows: bfloat16 [16, 4096, 2048], P('ep', 'seq'), may hold values from -6 to 6
- value_rows: bfloat16 [16, 4096, 2048], P('ep', 'seq'), may hold values from -6 to 6
- residual: bfloat16 [16, 4096, 2048], P('ep', 'seq'), may hold values from -6 to 6
- state_start: float32 [16, 16, 128, 128], P('ep'), may hold values from -192 to 192
- head_gain: float32 [2048], replicated, may hold values from 0.25 to 1.75
- ffn_gain: float32 [2048], replicated, may hold values from 0.25 to 1.75
- routes: int32 [16, 4096, 6], P('ep', 'seq'), may hold values from 0 to 15, all different within a row; in each aligned block of 128 rows (0 to 127, 128 to 255, ..., all dimensions but the last counted through in order) at most 50 rows name the same one
- route_gates: float32 [16, 4096, 6], P('ep', 'seq'), may hold values from 0.1 to 1
- gate_weight: bfloat16 [16, 2048, 704], P('ep', 'seq'), may hold values from -0.125 to 0.125
- up_weight: bfloat16 [16, 2048, 704], P('ep', 'seq'), may hold values from -0.125 to 0.125
- down_weight: bfloat16 [16, 704, 2048], P('ep', None, 'seq'), may hold values from -0.21875 to 0.21875
Outputs:
- layer_out: bfloat16 [16, 4096, 2048], P('ep', 'seq')
The draws below stay inside these ranges and needn't reach their ends.
Inputs may be any that keep to these rules, and one draw needn't show every extreme that they name: `routes`: each position names 6 different experts. Among the positions of one device (aligned blocks of 128 positions) no expert is named more than 50 times, a bound that some block reaches.
All inputs are finite; a program needn't handle non-finite values.
Results may differ from the reference program's by a relative error of at most 0.015.
Values may be sent and summed in bfloat16 or wider, within the bound.
A program may use at most 128 MiB of HBM per device.

```python
import math
import jax
import jax.numpy as jnp
import numpy as np
from jax import lax

D = 2048
HEADS = 16
HEAD_DIM = 128
HID = 704
EXPERTS = 16
TOP = 6
TOK_DEV = 128
CAP = 50
SEQS = 16
LENGTH = 4096
N_SEQ = 32


def block_scale(key, shape, cuts, smallest, largest):
    loudness, own = 1.0, jax.random.fold_in(key, 6)
    for axis_at, shards_of in cuts:
        draws = jnp.exp(jax.random.uniform(jax.random.fold_in(own, axis_at), (shards_of,), jnp.float32, smallest / len(cuts), largest / len(cuts)))
        loudness = loudness * jnp.repeat(draws, shape[axis_at] // shards_of).reshape([-1 if axis == axis_at else 1 for axis in range(len(shape))])
    return loudness


def shared_out(own_key, own, number, rows, number_of, top, bound, slope):
    order = jax.random.permutation(own_key, number_of)
    heavy_load, common = load_shares(number_of, rows * top, bound, slope, True), load_shares(number_of, rows * top, bound, slope, False)
    places = jnp.arange(number_of)

    def named(sizes, turn):
        used = int((sizes > 0).sum())
        fixed = max(1, used // 4)
        passed = fixed + (places - fixed + turn * (used - fixed)) % max(1, number_of - fixed)
        return jnp.zeros((number_of,), jnp.int32).at[order[jnp.where(places < fixed, places, passed)]].set(jnp.asarray(sizes, jnp.int32))

    sizes = jnp.where(number % 4 == 0, named(heavy_load, number // 4), named(common, number - number // 4 - 1))
    mixed = jax.random.permutation(jax.random.fold_in(own, 3), number_of)
    source_of, taker = mixed[0:number_of // 2 * 2:2], mixed[1:number_of // 2 * 2:2]
    margin = jnp.minimum(sizes[source_of] - 1, bound - sizes[taker]) // 2
    margin = jnp.where((source_of == order[0]) | (taker == order[0]) | (sizes[taker] == 0), 0, jnp.maximum(margin, 0))
    passed = jax.random.randint(jax.random.fold_in(own, 4), (number_of // 2,), 0, 1 << 20) % (margin + 1)
    sizes = sizes.at[source_of].add(-passed).at[taker].add(passed)
    members = jnp.searchsorted(jnp.cumsum(sizes), jnp.arange(rows * top), side="right").astype(jnp.int32)
    table = members.reshape(top, rows).T
    table = table[jax.random.permutation(jax.random.fold_in(own, 1), rows)]
    turn = jax.random.randint(jax.random.fold_in(own, 2), (rows, 1), 0, top)
    return jnp.take_along_axis(table, (jnp.arange(top)[None, :] + turn) % top, axis=1)


def load_shares(number_of, total, reach, slope, full):
    portions = [(1 << 20) // math.isqrt(rank ** slope) + 1 for rank in range(1, number_of + 1)]
    largest = reach if full else min(reach, max(-(-total // number_of), total * portions[0] // sum(portions)))
    least = 1 if total - largest >= number_of - 1 else 0
    holding, rest = [largest] + [least] * (number_of - 1), total - largest - least * (number_of - 1)
    while rest > 0:
        movable = [i for i in range(1, number_of) if holding[i] < largest] or [i for i in range(1, number_of) if holding[i] < reach]
        mass, remaining = sum([portions[i] for i in movable]), rest
        for i in movable:
            more = min(reach - holding[i], max(1, remaining * portions[i] // mass), rest)
            holding[i] = holding[i] + more
            rest = rest - more
    return np.array(holding)


def centred(rng, shape, spread, limit, shards=(), held_as=jnp.bfloat16):
    loudness = block_scale(rng, shape, shards, -0.22, 0.18) if shards else 1.0
    entries = jax.random.normal(rng, shape, jnp.float32) * spread * loudness
    return jnp.minimum(jnp.maximum(entries, -limit), limit).astype(held_as)


def setup_inputs(seed: int = 0) -> dict:
    streams_of = jax.random.split(jax.random.key(seed), 13)
    queries = centred(streams_of[0], (SEQS, LENGTH, D), 1.0, 6.0, ((0, 16), (1, 32)))
    key_rows = centred(streams_of[1], (SEQS, LENGTH, D), 1.0, 6.0, ((0, 16), (1, 32)))
    value_rows = centred(streams_of[2], (SEQS, LENGTH, D), 1.0, 6.0, ((0, 16), (1, 32)))
    residual = centred(streams_of[3], (SEQS, LENGTH, D), 1.0, 6.0, ((0, 16), (1, 32)))
    state_start = centred(streams_of[4], (SEQS, HEADS, HEAD_DIM, HEAD_DIM), (0.5 * LENGTH ** 0.5), 192.0, ((0, 16),), jnp.float32)
    head_gain = jnp.clip(1.0 + 0.15 * jax.random.normal(streams_of[5], (D,), jnp.float32), 0.25, 1.75)
    ffn_gain = jnp.clip(1.0 + 0.15 * jax.random.normal(streams_of[6], (D,), jnp.float32), 0.25, 1.75)
    routes_keys = jax.random.split(jax.random.fold_in(streams_of[7], 1), SEQS * LENGTH // TOK_DEV)
    routes_turns = jax.random.permutation(jax.random.fold_in(streams_of[7], 3), SEQS * LENGTH // TOK_DEV)
    routes = jax.vmap(lambda own, number: shared_out(jax.random.fold_in(streams_of[7], 2), own, number, TOK_DEV, EXPERTS, TOP, CAP, 2))(routes_keys, routes_turns).reshape((SEQS, LENGTH, TOP))
    route_gates = jnp.clip(0.1 + 0.9 * jax.random.uniform(streams_of[8], (SEQS, LENGTH, TOP), jnp.float32) ** block_scale(streams_of[8], (SEQS, LENGTH, TOP), ((0, 16), (1, 32)), -0.2, 0.2), 0.1, 1.0)
    gate_weight = centred(streams_of[9], (EXPERTS, D, HID), D ** -0.5, 0.125, ((0, 16), (1, 32)))
    up_weight = centred(streams_of[10], (EXPERTS, D, HID), D ** -0.5, 0.125, ((0, 16), (1, 32)))
    down_weight = centred(streams_of[11], (EXPERTS, HID, D), HID ** -0.5, 0.21875, ((0, 16), (2, 32)))
    return {"queries": queries, "key_rows": key_rows, "value_rows": value_rows, "residual": residual, "state_start": state_start, "head_gain": head_gain, "ffn_gain": ffn_gain, "routes": routes, "route_gates": route_gates, "gate_weight": gate_weight, "up_weight": up_weight, "down_weight": down_weight}


def route_slots(block_routes):
    chosen = (block_routes[:, None] == jnp.arange(EXPERTS, dtype=jnp.int32)[None, :]).astype(jnp.int32)
    counts = jnp.cumsum(chosen, axis=0) - 1
    return lax.optimization_barrier(jnp.sum(chosen * counts, axis=1)).astype(jnp.int32)

def silu_gate(gate_sum, up_sum):
    return gate_sum / (1.0 + jnp.exp(-gate_sum)) * up_sum

def reference(queries, key_rows, value_rows, residual, state_start, head_gain, ffn_gain, routes, route_gates, gate_weight, up_weight, down_weight):
    highest = lax.Precision.HIGHEST
    causal = jnp.arange(TOK_DEV, dtype=jnp.int32)[:, None] >= jnp.arange(TOK_DEV, dtype=jnp.int32)[None, :]

    def attend_block(state_before, block):
        query_heads, key_heads, value_heads = block
        query_wide = query_heads.astype(jnp.float32)
        key_wide = key_heads.astype(jnp.float32)
        value_wide = value_heads.astype(jnp.float32)
        from_state = jnp.einsum('thd,hde->the', query_wide, state_before, precision=highest)
        scores = jnp.einsum('thd,shd->hts', query_wide, key_wide, precision=highest)
        scores = jnp.where(causal[None], scores, 0.0).astype(jnp.bfloat16)
        in_block = jnp.einsum('hts,she->the', scores.astype(jnp.float32), value_wide, precision=highest)
        state_after = state_before + jnp.einsum('thd,the->hde', key_wide, value_wide, precision=highest)
        return (state_after, from_state + in_block)

    def run_expert(packed_expert):
        rows, gate_part, up_part, down_part = packed_expert
        gate_sum = jnp.dot(rows, gate_part, preferred_element_type=jnp.float32)
        up_sum = jnp.dot(rows, up_part, preferred_element_type=jnp.float32)
        hidden = silu_gate(gate_sum, up_sum).astype(jnp.bfloat16)
        return jnp.dot(hidden, down_part, preferred_element_type=jnp.float32).astype(jnp.bfloat16)

    def one_sequence(packed):
        query_seq, key_seq, value_seq, resid_seq, state_seq, route_seq, weight_seq = packed
        blocked = (query_seq.reshape(N_SEQ, TOK_DEV, HEADS, HEAD_DIM), key_seq.reshape(N_SEQ, TOK_DEV, HEADS, HEAD_DIM), value_seq.reshape(N_SEQ, TOK_DEV, HEADS, HEAD_DIM))
        final_state, attended = lax.scan(attend_block, state_seq, blocked)
        attended = attended.reshape(LENGTH, HEADS, HEAD_DIM)
        head_scale = lax.rsqrt(lax.optimization_barrier(jnp.mean(attended * attended, axis=-1, keepdims=True)) + 1e-05)
        head_normed = (attended * head_scale).reshape(LENGTH, D) * head_gain
        mixed_rows = (resid_seq.astype(jnp.float32) + head_normed).astype(jnp.bfloat16)
        mixed_rows = lax.optimization_barrier(mixed_rows)
        mixed_wide = mixed_rows.astype(jnp.float32)
        row_scale = lax.rsqrt(lax.optimization_barrier(jnp.mean(mixed_wide * mixed_wide, axis=-1, keepdims=True)) + 1e-05)
        ffn_in = (mixed_wide * row_scale * ffn_gain).astype(jnp.bfloat16)
        flat_routes = route_seq.reshape(N_SEQ, TOK_DEV * TOP)
        slot_rank = jax.vmap(route_slots)(flat_routes)
        block_index = jnp.arange(N_SEQ, dtype=jnp.int32)[:, None]
        position = (flat_routes * (N_SEQ * CAP) + block_index * CAP + slot_rank).reshape(-1)
        token_index = (block_index * TOK_DEV + jnp.arange(TOK_DEV * TOP, dtype=jnp.int32)[None, :] // TOP).reshape(-1)
        source = jnp.zeros((EXPERTS * N_SEQ * CAP,), jnp.int32).at[position].set(token_index)
        filled = jnp.zeros((EXPERTS * N_SEQ * CAP,), jnp.bool_).at[position].set(True)
        buffers = jnp.where(filled[:, None], ffn_in[source], jnp.zeros((), jnp.bfloat16)).reshape(EXPERTS, N_SEQ * CAP, D)
        outputs = lax.map(run_expert, (buffers, gate_weight, up_weight, down_weight))
        picked = outputs.reshape(EXPERTS * N_SEQ * CAP, D)[position].reshape(LENGTH, TOP, D)
        expert_mix = lax.optimization_barrier(jnp.sum(weight_seq[:, :, None] * picked.astype(jnp.float32), axis=1))
        return (mixed_wide + expert_mix).astype(jnp.bfloat16)
    return lax.map(one_sequence, (queries, key_rows, value_rows, residual, state_start, routes, route_gates))
```

```python
import functools

import jax
import jax.numpy as jnp
from jax import lax
from jax.experimental import pallas as pl
from jax.experimental.pallas import tpu as pltpu
from jax.sharding import PartitionSpec as P

D = 2048
HALF = 1024
HEADS = 16
HD = 128
HID = 704
EXPERTS = 16
TOP = 6
T = 128
NX, NZ, NY = 4, 8, 8
MESH = pl.DeviceIdType.MESH
F32 = jnp.float32
BF16 = jnp.bfloat16
HIGH = lax.Precision.HIGHEST
TN = (((0,), (0,)), ((), ()))
NT = (((1,), (1,)), ((), ()))
NN = (((1,), (0,)), ((), ()))


def dot(a, b, dims=NN, precision=None):
    return lax.dot_general(a, b, dims, precision=precision, preferred_element_type=F32)


def place():
    seq, ep = lax.axis_index("seq"), lax.axis_index("ep")
    return seq // NZ, lax.rem(seq, NZ), ep // 2, lax.rem(ep, 2)


def ring(at, step, size):
    return lax.rem(at + step + size, size)


def remote(src, dst, send, recv, device):
    return pltpu.make_async_remote_copy(
        src_ref=src, dst_ref=dst, send_sem=send, recv_sem=recv, device_id=device, device_id_type=MESH
    )


def greet(devices):
    barrier = pltpu.get_barrier_semaphore()
    for device in devices:
        pl.semaphore_signal(barrier, inc=1, device_id=device, device_id_type=MESH)
    pl.semaphore_wait(barrier, len(devices))


def cols(h):
    return pl.ds(pl.multiple_of(h * HD, HD), HD)


class YGather:
    def __init__(self, at, units, near, sib_send, sib_recv, send, recv):
        self.x, self.z, self.y, self.c = at
        self.seq = self.x * NZ + self.z
        self.units, self.sends, self.recvs = units, send, recv
        self.sib_send, self.sib_recv = sib_send, sib_recv
        self.pending = []
        del near

    def hop(self, way, w, k):
        block = ring(self.y, -(1 - 2 * way) * (k - 1), NY)
        ref = self.units[w].at[block, self.c]
        to = (self.seq, ring(self.y, 1 - 2 * way, NY) * 2 + self.c)
        n = (way * len(self.units) + w) * 4 + k - 1
        return remote(ref, ref, self.sends.at[n], self.recvs.at[n], to)

    def landed(self, way, w, k):
        block = ring(self.y, -(1 - 2 * way) * k, NY)
        ref = self.units[w].at[block, self.c]
        n = (way * len(self.units) + w) * 4 + k - 1
        return remote(ref, ref, self.sends.at[n], self.recvs.at[n], (self.seq, self.y * 2 + 1 - self.c))

    def across(self, way, w, k, core):
        block = ring(self.y, -(1 - 2 * way) * k, NY)
        ref = self.units[w].at[block, core]
        n = (way * len(self.units) + w) * 5 + k
        return remote(ref, ref, self.sib_send.at[n], self.sib_recv.at[n], (self.seq, self.y * 2 + 1 - self.c))

    def last(self, way, w):
        return way == w % 2

    def start(self, w):
        for way in (0, 1):
            self.hop(way, w, 1).start()
            self.pending.append((way, w, 1))
        self.across(0, w, 0, self.c).start()
        self.crossed = getattr(self, "crossed", []) + [(0, w, 0)]

    def step(self, w, k):
        for way in (0, 1):
            if k == 4 and not self.last(way, w):
                continue
            self.landed(way, w, k).wait_recv()
            if k < 3 or (k == 3 and self.last(way, w)):
                self.hop(way, w, k + 1).start()
                self.pending.append((way, w, k + 1))
            self.across(way, w, k, self.c).start()
            self.crossed.append((way, w, k))

    def finish(self):
        for way, w, k in self.crossed:
            self.across(way, w, k, 1 - self.c).wait_recv()
        for way, w, k in self.pending:
            self.hop(way, w, k).wait_send()
        for way, w, k in self.crossed:
            self.across(way, w, k, self.c).wait_send()


def attend_kernel(
    q, k, v, res, s0, hg, fg, gt,
    rows, gates, mixed,
    mine, parts, back, totals, prior, base,
    z1s, z1r, xs, xr, z2s, z2r, ysend, yrecv, ssend, srecv,
):
    at = x, z, y, c = place()
    seq, ep = x * NZ + z, y * 2 + c
    per = HEADS // NZ
    greet(
        [(x * NZ + ring(z, o, NZ), ep) for o in range(1, NZ)]
        + [(ring(x, o, NX) * NZ + z, ep) for o in range(1, NX)]
        + [(seq, ring(y, o, NY) * 2 + c) for o in (1, -1)]
        + [(seq, y * 2 + 1 - c)]
    )
    gather = YGather(at, [rows.at[:, :, 0], rows.at[:, :, 1], gates], None, ssend, srecv, ysend, yrecv)
    gates[y, c] = gt[...]
    gather.start(2)

    for o in list(range(1, NZ)) + [0]:
        owner = ring(z, o, NZ)
        for i in range(per):
            at_cols = cols(owner * per + i)
            state = dot(k[:, at_cols], v[:, at_cols], TN).astype(BF16)
            if o:
                mine[o, i] = state
            else:
                parts[z, i] = state
        if o:
            remote(mine.at[o], parts.at[z], z1s.at[o], z1r.at[o], (x * NZ + owner, ep)).start()

    causal = lax.broadcasted_iota(jnp.int32, (T, T), 0) >= lax.broadcasted_iota(jnp.int32, (T, T), 1)

    @pl.loop(0, HEADS)
    def _(h):
        at_cols = cols(h)
        qh, kh = q[:, at_cols], k[:, at_cols]
        scores = jnp.where(causal, dot(qh, kh, NT), 0.0).astype(BF16)
        base[:, at_cols] = dot(scores, v[:, at_cols]) + dot(qh.astype(F32), s0[h], precision=HIGH)

    gather.step(2, 1)
    for o in range(1, NZ):
        frm = ring(z, -o, NZ)
        remote(mine.at[o], parts.at[frm], z1s.at[o], z1r.at[o], (x * NZ + frm, ep)).wait_recv()
    total = jnp.zeros((per, HD, HD), F32)
    for o in range(NZ):
        total = total + parts[o].astype(F32)
    totals[x] = total.astype(BF16)
    for o in range(1, NX):
        remote(totals.at[x], totals.at[x], xs.at[o], xr.at[o], (ring(x, o, NX) * NZ + z, ep)).start()
    gather.step(2, 2)
    for o in range(1, NX):
        frm = ring(x, -o, NX)
        remote(totals.at[frm], totals.at[frm], xs.at[o], xr.at[o], (frm * NZ + z, ep)).wait_recv()
    state = jnp.zeros((per, HD, HD), F32)
    for o in range(NX - 1):
        state = state + jnp.where(o < x, totals[o].astype(F32), 0.0)
    for o in range(NZ):
        back[o] = state.astype(BF16)
        state = state + parts[o].astype(F32)
    for o in range(1, NZ):
        to = ring(z, o, NZ)
        remote(back.at[to], prior.at[z], z2s.at[o], z2r.at[o], (x * NZ + to, ep)).start()
    prior[z] = back[z]
    gather.step(2, 3)

    squares = jnp.zeros((T, 1), F32)
    for o in range(NZ):
        owner = ring(z, -o, NZ)
        if o:
            remote(back.at[owner], prior.at[owner], z2s.at[o], z2r.at[o], (x * NZ + owner, ep)).wait_recv()
        for i in range(per):
            at_cols = cols(owner * per + i)
            attended = base[:, at_cols] + dot(q[:, at_cols], prior[owner, i])
            scale = lax.rsqrt(jnp.mean(attended * attended, axis=-1, keepdims=True) + 1e-05)
            normed = attended * scale * hg[:, at_cols]
            row = (res[:, at_cols].astype(F32) + normed).astype(BF16)
            mixed[:, at_cols] = row
            wide = row.astype(F32)
            squares = squares + jnp.sum(wide * wide, axis=-1, keepdims=True)
    row_scale = lax.rsqrt(squares / D + 1e-05)
    for w in (0, 1):
        half = slice(w * HALF, (w + 1) * HALF)
        rows[y, c, w] = (mixed[:, half].astype(F32) * row_scale * fg[:, half]).astype(BF16)
        gather.start(w)
    gather.step(2, 4)
    for k_ in (1, 2, 3, 4):
        for w in (0, 1):
            gather.step(w, k_)
    gather.finish()
    for o in range(1, NZ):
        to = ring(z, o, NZ)
        remote(mine.at[o], parts.at[z], z1s.at[o], z1r.at[o], (x * NZ + to, ep)).wait_send()
        remote(back.at[to], prior.at[z], z2s.at[o], z2r.at[o], (x * NZ + to, ep)).wait_send()
    for o in range(1, NX):
        remote(totals.at[x], totals.at[x], xs.at[o], xr.at[o], (ring(x, o, NX) * NZ + z, ep)).wait_send()


ORDER = (4, 3, -3, 2, -2, 1, -1, 0)


def expert_kernel(
    rows, gates, mixed, gu, dt,
    out,
    hidden, own, sibout, sibin, ringout, ringin, finout, finin,
    ssend, srecv, rsend, rrecv, fsend, frecv,
):
    x, z, y, c = place()
    seq, ep = x * NZ + z, y * 2 + c
    sibling = (seq, y * 2 + 1 - c)
    greet([(seq, ring(y, o, NY) * 2 + c) for o in (1, -1)] + [sibling])
    pick = (lax.broadcasted_iota(jnp.int32, (EXPERTS, HD), 0) == ep).astype(F32)
    low = lax.broadcasted_iota(jnp.int32, (2 * T, HD), 1) < HID % HD

    def silu(gate_sum, up_sum):
        return gate_sum / (1.0 + jnp.exp(-gate_sum)) * up_sum

    def hop(way, j, t):
        n = (way * 4 + j) * 2 + t
        to = (seq, ring(y, 1 - 2 * way, NY) * 2 + c)
        return remote(ringout.at[way, j, t], ringin.at[way, j, t], rsend.at[n], rrecv.at[n], to)

    def cross(n):
        return remote(sibout.at[n], sibin.at[n], ssend.at[n], srecv.at[n], sibling)

    started = []
    for n, off in enumerate(ORDER):
        block = ring(y, off, NY)
        left = rows[block, :, 0].reshape(2 * T, HALF)
        right = rows[block, :, 1].reshape(2 * T, HALF)

        @pl.loop(0, 5)
        def _(i):
            tile = pl.ds(pl.multiple_of(i * 256, 256), 256)
            both = dot(left, gu[:HALF, tile]) + dot(right, gu[HALF:, tile])
            hidden[:, cols(i)] = silu(both[:, :HD], both[:, HD:]).astype(BF16)

        both = dot(left, gu[:HALF, 1280:]) + dot(right, gu[HALF:, 1280:])
        turned = pltpu.roll(both, HD // 2, 1)
        hidden[:, 640:] = jnp.where(low, silu(both, turned), 0.0).astype(BF16)
        gate = jnp.concatenate([dot(gates[block, t], pick, TN, HIGH) for t in (0, 1)], axis=0)
        gate = jnp.concatenate([gate, gate], axis=1)

        @pl.loop(0, 4)
        def _(i):
            tile = pl.ds(pl.multiple_of(i * 256, 256), 256)
            part = dot(hidden[...], dt[1 - c, tile, :], NT) * gate
            sibout[n, :, :, tile] = part.astype(BF16).reshape(2, T, 256)

        cross(n).start()

        @pl.loop(0, 4)
        def _(i):
            tile = pl.ds(pl.multiple_of(i * 256, 256), 256)
            own[:, :, tile] = (dot(hidden[...], dt[c, tile, :], NT) * gate).reshape(2, T, 256)

        cross(n).wait_recv()
        way = 0 if off >= 0 else 1
        for t in (0, 1):
            total = own[t] + sibin[n, t].astype(F32)
            if off == 4:
                ringout[t, 3, t] = total.astype(BF16)
                hop(t, 3, t).start()
                started.append((t, 3, t))
                continue
            j = abs(off)
            for came in (0, 1) if off == 0 else (way,):
                if j == 3 and came != t:
                    continue
                hop(came, j, t).wait_recv()
                total = total + ringin[came, j, t].astype(F32)
            if off:
                ringout[way, j - 1, t] = total.astype(BF16)
                hop(way, j - 1, t).start()
                started.append((way, j - 1, t))
            else:
                own[t] = total

    finout[...] = own[1 - c].astype(BF16)
    final = remote(finout, finin, fsend.at[0], frecv.at[0], sibling)
    final.start()
    mine = pl.ds(pl.multiple_of(c * HALF, HALF), HALF)
    other = pl.ds(pl.multiple_of((1 - c) * HALF, HALF), HALF)
    out[:, mine] = (mixed[:, mine].astype(F32) + own[c]).astype(BF16)
    final.wait()
    out[:, other] = (mixed[:, other].astype(F32) + finin[...].astype(F32)).astype(BF16)
    for way, j, t in started:
        hop(way, j, t).wait_send()
    for n in range(8):
        cross(n).wait_send()


VMEM = pl.BlockSpec(memory_space=pltpu.VMEM)
DMA = pltpu.SemaphoreType.DMA


def shards(q, k, v, res, s0, hg, fg, routes, route_gates, gate_w, up_w, down_w):
    experts = jnp.arange(EXPERTS, dtype=jnp.int32)[:, None]
    chosen, weight = routes[0].T, route_gates[0].T
    gt = jnp.zeros((EXPERTS, T), F32)
    for i in range(TOP):
        gt = gt + jnp.where(chosen[i][None] == experts, weight[i][None], 0.0)
    pieces = []
    for i in range(0, HID, HD):
        pieces += [gate_w[0][:, i : i + HD], up_w[0][:, i : i + HD]]
    gu = lax.all_gather(jnp.concatenate(pieces, axis=1), "seq", axis=0, tiled=True)
    dt = jnp.pad(down_w[0].T, ((0, 0), (0, 768 - HID)))
    dt = lax.all_gather(dt, "seq", axis=0, tiled=True)

    rows, gates, mixed = pl.pallas_call(
        attend_kernel,
        out_shape=(
            jax.ShapeDtypeStruct((NY, 2, 2, T, HALF), BF16),
            jax.ShapeDtypeStruct((NY, 2, EXPERTS, T), F32),
            jax.ShapeDtypeStruct((T, D), BF16),
        ),
        in_specs=[VMEM] * 8,
        out_specs=(VMEM,) * 3,
        scratch_shapes=[
            pltpu.VMEM((NZ, 2, HD, HD), BF16),
            pltpu.VMEM((NZ, 2, HD, HD), BF16),
            pltpu.VMEM((NZ, 2, HD, HD), BF16),
            pltpu.VMEM((NX, 2, HD, HD), BF16),
            pltpu.VMEM((NZ, 2, HD, HD), BF16),
            pltpu.VMEM((T, D), F32),
            DMA((NZ,)), DMA((NZ,)), DMA((NX,)), DMA((NX,)), DMA((NZ,)), DMA((NZ,)),
            DMA((24,)), DMA((24,)), DMA((30,)), DMA((30,)),
        ],
        compiler_params=pltpu.CompilerParams(
            collective_id=0, has_side_effects=True, vmem_limit_bytes=40 * 2**20
        ),
        cost_estimate=pl.CostEstimate(flops=500_000_000, bytes_accessed=300_000_000, transcendentals=0),
        name="attend",
    )(q[0], k[0], v[0], res[0], s0[0], hg[None], fg[None], gt)

    out = pl.pallas_call(
        expert_kernel,
        out_shape=jax.ShapeDtypeStruct((T, D), BF16),
        in_specs=[VMEM] * 5,
        out_specs=VMEM,
        scratch_shapes=[
            pltpu.VMEM((2 * T, 768), BF16),
            pltpu.VMEM((2, T, HALF), F32),
            pltpu.VMEM((8, 2, T, HALF), BF16),
            pltpu.VMEM((8, 2, T, HALF), BF16),
            pltpu.VMEM((2, 4, 2, T, HALF), BF16),
            pltpu.VMEM((2, 4, 2, T, HALF), BF16),
            pltpu.VMEM((T, HALF), BF16),
            pltpu.VMEM((T, HALF), BF16),
            DMA((8,)), DMA((8,)), DMA((16,)), DMA((16,)), DMA((1,)), DMA((1,)),
        ],
        compiler_params=pltpu.CompilerParams(
            collective_id=1, has_side_effects=True, vmem_limit_bytes=56 * 2**20
        ),
        name="experts",
    )(rows, gates, mixed, gu, dt.reshape(2, HALF, 768))
    return out[None]


def solution(mesh):
    placed = (
        P("ep", "seq", None),
        P("ep", "seq", None),
        P("ep", "seq", None),
        P("ep", "seq", None),
        P("ep", None, None, None),
        P(),
        P(),
        P("ep", "seq", None),
        P("ep", "seq", None),
        P("ep", "seq", None),
        P("ep", "seq", None),
        P("ep", None, "seq"),
    )
    return jax.shard_map(
        shards, mesh=mesh, in_specs=placed, out_specs=P("ep", "seq", None), check_vma=False
    )
```

```python
import functools

import jax
import jax.numpy as jnp
from jax import lax
from jax.experimental import pallas as pl
from jax.experimental.pallas import tpu as pltpu
from jax.sharding import PartitionSpec as P

D = 2048
HALF = 1024
HEADS = 16
HD = 128
HID = 704
EXPERTS = 16
TOP = 6
T = 128
NX, NZ, NY = 4, 8, 8
MESH = pl.DeviceIdType.MESH
F32 = jnp.float32
BF16 = jnp.bfloat16
HIGH = lax.Precision.HIGHEST
TN = (((0,), (0,)), ((), ()))
NT = (((1,), (1,)), ((), ()))
NN = (((1,), (0,)), ((), ()))


def dot(a, b, dims=NN, precision=None):
    return lax.dot_general(a, b, dims, precision=precision, preferred_element_type=F32)


def place():
    seq, ep = lax.axis_index("seq"), lax.axis_index("ep")
    return seq // NZ, lax.rem(seq, NZ), ep // 2, lax.rem(ep, 2)


def ring(at, step, size):
    return lax.rem(at + step + size, size)


def remote(src, dst, send, recv, device):
    return pltpu.make_async_remote_copy(
        src_ref=src, dst_ref=dst, send_sem=send, recv_sem=recv, device_id=device, device_id_type=MESH
    )


def greet(devices):
    barrier = pltpu.get_barrier_semaphore()
    for device in devices:
        pl.semaphore_signal(barrier, inc=1, device_id=device, device_id_type=MESH)
    pl.semaphore_wait(barrier, len(devices))


def cols(h):
    return pl.ds(pl.multiple_of(h * HD, HD), HD)


class Ring:
    def __init__(self, at, n, device, units, send, recv):
        self.at, self.n, self.device, self.units = at, n, device, units
        self.send, self.recv, self.started = send, recv, []

    def block(self, way, k):
        return ring(self.at, -(1 - 2 * way) * k, self.n)

    def copy(self, way, w, k, block):
        ref = self.units[w](block)
        i = (way * len(self.units) + w) * (self.n // 2) + k - 1
        to = self.device(ring(self.at, 1 - 2 * way, self.n))
        return remote(ref, ref, self.send.at[i], self.recv.at[i], to)

    def ways(self, w, k):
        return (0, 1) if k < self.n // 2 else (w % 2,)

    def hop(self, way, w, k):
        self.copy(way, w, k, self.block(way, k - 1)).start()
        self.started.append((way, w, k))

    def start(self, w):
        for way in (0, 1):
            self.hop(way, w, 1)

    def step(self, w, k):
        for way in self.ways(w, k):
            self.copy(way, w, k, self.block(way, k)).wait_recv()
            if k < self.n // 2 and way in self.ways(w, k + 1):
                self.hop(way, w, k + 1)

    def sent(self):
        for way, w, k in self.started:
            self.copy(way, w, k, self.block(way, k - 1)).wait_send()


class PairRing(Ring):
    def __init__(self, at, n, device, units, send, recv, core, sibling, cross_send, cross_recv):
        self.mine = [functools.partial(unit, core=core) for unit in units]
        self.other = [functools.partial(unit, core=1 - core) for unit in units]
        super().__init__(at, n, device, self.mine, send, recv)
        self.sibling, self.cross_send, self.cross_recv = sibling, cross_send, cross_recv
        self.crossed = []

    def across(self, way, w, k, units):
        ref = units[w](self.block(way, k))
        i = (way * len(units) + w) * (self.n // 2 + 1) + k
        return remote(ref, ref, self.cross_send.at[i], self.cross_recv.at[i], self.sibling)

    def cross(self, way, w, k):
        self.across(way, w, k, self.mine).start()
        self.crossed.append((way, w, k))

    def start(self, w):
        super().start(w)
        self.cross(0, w, 0)

    def step(self, w, k):
        super().step(w, k)
        for way in self.ways(w, k):
            self.cross(way, w, k)

    def came_across(self):
        for way, w, k in self.crossed:
            self.across(way, w, k, self.other).wait_recv()

    def sent(self):
        super().sent()
        for way, w, k in self.crossed:
            self.across(way, w, k, self.mine).wait_send()


ORDER = (4, 3, -3, 2, -2, 1, -1, 0)
NEAR = (0, 1, -1, 2, -2, 3, -3, 4)


def kernel(
    q_in, k_in, v_in, res_in, s0_in, gu_in, dt_in, hg, fg, gt,
    out,
    q, k, v, res, s0, gu, dt, rows, gates, mixed,
    mine, parts, back, totals, prior, base,
    hidden, own, sibout, sibin, ringout, ringin, finout, finin,
    load, z1s, z1r, xs, xr, z2s, z2r, ys, yr, ycs, ycr, gs, gr, gcs, gcr,
    gzs, gzr, gxs, gxr, dxs, dxr, dzs, dzr, ss, sr, rs, rr, fs, fr,
):
    x, z, y, c = place()
    seq, ep = x * NZ + z, y * 2 + c
    per = HEADS // NZ
    sibling = (seq, y * 2 + 1 - c)
    loads = [
        pltpu.make_async_copy(src, dst, load.at[i])
        for i, (src, dst) in enumerate(
            [(k_in, k), (v_in, v), (gu_in, gu.at[x, z]), (dt_in, dt.at[x, z]), (q_in, q), (s0_in, s0), (res_in, res)]
        )
    ]
    for one in loads:
        one.start()
    greet(
        [(x * NZ + ring(z, o, NZ), ep) for o in range(1, NZ)]
        + [(ring(x, o, NX) * NZ + z, ep) for o in range(1, NX)]
        + [(seq, ring(y, o, NY) * 2 + c) for o in (1, -1)]
        + [sibling]
    )

    def on_x(place):
        return place * NZ + z, ep

    def on_y(place):
        return seq, place * 2 + c

    def on_z(place):
        return x * NZ + place, ep

    tokens = PairRing(
        y, NY, on_y, [lambda b, core, w=w: rows.at[b, core, w] for w in (0, 1)], ys, yr, c, sibling, ycs, ycr
    )
    gate_ring = PairRing(y, NY, on_y, [lambda b, core: gates.at[b, core]], gs, gr, c, sibling, gcs, gcr)
    up_z = Ring(z, NZ, on_z, [lambda b, w=w: gu.at[x, b, pl.ds(w * 32, 32)] for w in (0, 1)], gzs, gzr)
    up_x = Ring(x, NX, on_x, [lambda b, o=o: gu.at[b, ring(z, o, NZ)] for o in NEAR], gxs, gxr)
    down_z = Ring(z, NZ, on_z, [lambda b, w=w: dt.at[pl.ds(w * 2, 2), b] for w in (0, 1)], dzs, dzr)

    def down_x(o, frm):
        ref = dt.at[frm, z]
        return remote(ref, ref, dxs.at[o], dxr.at[o], on_x(ring(x, o, NX)))

    gates[y, c] = gt[...]
    gate_ring.start(0)

    loads[0].wait()
    loads[1].wait()
    for o in list(range(1, NZ)) + [0]:
        owner = ring(z, o, NZ)
        for i in range(per):
            at_cols = cols(owner * per + i)
            state = dot(k[:, at_cols], v[:, at_cols], TN).astype(BF16)
            if o:
                mine[o, i] = state
            else:
                parts[z, i] = state
        if o:
            remote(mine.at[o], parts.at[z], z1s.at[o], z1r.at[o], on_z(owner)).start()
    loads[2].wait()
    for w in (0, 1):
        up_z.start(w)
    up_x.start(0)
    loads[3].wait()
    for o in range(1, NX):
        down_x(o, x).start()

    causal = lax.broadcasted_iota(jnp.int32, (T, T), 0) >= lax.broadcasted_iota(jnp.int32, (T, T), 1)
    loads[4].wait()
    loads[5].wait()

    @pl.loop(0, HEADS)
    def _(h):
        at_cols = cols(h)
        qh, kh = q[:, at_cols], k[:, at_cols]
        scores = jnp.where(causal, dot(qh, kh, NT), 0.0).astype(BF16)
        base[:, at_cols] = dot(scores, v[:, at_cols]) + dot(qh.astype(F32), s0[h], precision=HIGH)

    def up_step(n):
        for w in (0, 1):
            up_z.step(w, n)
        for w, o in enumerate(NEAR):
            if abs(o) == n:
                up_x.start(w)

    gate_ring.step(0, 1)
    for o in range(1, NZ):
        frm = ring(z, -o, NZ)
        remote(mine.at[o], parts.at[frm], z1s.at[o], z1r.at[o], on_z(frm)).wait_recv()
    total = jnp.zeros((per, HD, HD), F32)
    for o in range(NZ):
        total = total + parts[o].astype(F32)
    totals[x] = total.astype(BF16)
    for o in range(1, NX):
        remote(totals.at[x], totals.at[x], xs.at[o], xr.at[o], on_x(ring(x, o, NX))).start()
    up_step(1)
    gate_ring.step(0, 2)
    for o in range(1, NX):
        frm = ring(x, -o, NX)
        remote(totals.at[frm], totals.at[frm], xs.at[o], xr.at[o], on_x(frm)).wait_recv()
    state = jnp.zeros((per, HD, HD), F32)
    for o in range(NX - 1):
        state = state + jnp.where(o < x, totals[o].astype(F32), 0.0)
    for o in range(NZ):
        back[o] = state.astype(BF16)
        state = state + parts[o].astype(F32)
    for o in range(1, NZ):
        to = ring(z, o, NZ)
        remote(back.at[to], prior.at[z], z2s.at[o], z2r.at[o], on_z(to)).start()
    prior[z] = back[z]
    up_step(2)
    gate_ring.step(0, 3)
    up_x.step(0, 1)
    for o in range(1, NX):
        down_x(o, ring(x, -o, NX)).wait_recv()
    loads[6].wait()

    squares = jnp.zeros((T, 1), F32)
    for o in range(NZ):
        owner = ring(z, -o, NZ)
        if o:
            remote(back.at[owner], prior.at[owner], z2s.at[o], z2r.at[o], on_z(owner)).wait_recv()
        for i in range(per):
            at_cols = cols(owner * per + i)
            attended = base[:, at_cols] + dot(q[:, at_cols], prior[owner, i])
            scale = lax.rsqrt(jnp.mean(attended * attended, axis=-1, keepdims=True) + 1e-05)
            normed = attended * scale * hg[:, at_cols]
            row = (res[:, at_cols].astype(F32) + normed).astype(BF16)
            mixed[:, at_cols] = row
            wide = row.astype(F32)
            squares = squares + jnp.sum(wide * wide, axis=-1, keepdims=True)
    row_scale = lax.rsqrt(squares / D + 1e-05)
    for w in (0, 1):
        half = slice(w * HALF, (w + 1) * HALF)
        rows[y, c, w] = (mixed[:, half].astype(F32) * row_scale * fg[:, half]).astype(BF16)
        tokens.start(w)
    up_step(3)
    for w in (0, 1):
        down_z.start(w)
    gate_ring.step(0, 4)
    up_step(4)
    for n in range(1, 5):
        for w in (0, 1):
            tokens.step(w, n)
            if n == 1:
                up_x.step(w + 1, 1)
                down_z.step(w, 1)
            else:
                if 2 * n + w - 1 < len(NEAR):
                    up_x.step(2 * n + w - 1, 1)
                up_x.step(2 * n + w - 4, 2)
                down_z.step(w, n)
    up_x.step(6, 2)
    up_x.step(7, 2)
    gate_ring.came_across()
    tokens.came_across()

    pick = (lax.broadcasted_iota(jnp.int32, (EXPERTS, HD), 0) == ep).astype(F32)
    low = lax.broadcasted_iota(jnp.int32, (2 * T, HD), 1) < HID % HD

    def silu(gate_sum, up_sum):
        return gate_sum / (1.0 + jnp.exp(-gate_sum)) * up_sum

    def hop(way, j, t):
        n = (way * 4 + j) * 2 + t
        to = on_y(ring(y, 1 - 2 * way, NY))
        return remote(ringout.at[way, j, t], ringin.at[way, j, t], rs.at[n], rr.at[n], to)

    def cross(n):
        return remote(sibout.at[n], sibin.at[n], ss.at[n], sr.at[n], sibling)

    def up_tile(left, right, tile):
        top = gu[0:2, :, :, tile].reshape(HALF, -1)
        bottom = gu[2:4, :, :, tile].reshape(HALF, -1)
        return dot(left, top) + dot(right, bottom)

    def down_tile(half, i):
        piece = dt[half * 2 + i // 2, pl.ds(lax.rem(i, 2) * 4, 4)]
        return dot(hidden[...], piece.reshape(256, 768), NT)

    started = []
    for n, off in enumerate(ORDER):
        block = ring(y, off, NY)
        left = rows[block, :, 0].reshape(2 * T, HALF)
        right = rows[block, :, 1].reshape(2 * T, HALF)

        @pl.loop(0, 5)
        def _(i):
            both = up_tile(left, right, pl.ds(pl.multiple_of(i * 256, 256), 256))
            hidden[:, cols(i)] = silu(both[:, :HD], both[:, HD:]).astype(BF16)

        both = up_tile(left, right, pl.ds(1280, HD))
        turned = pltpu.roll(both, HD // 2, 1)
        hidden[:, 640:] = jnp.where(low, silu(both, turned), 0.0).astype(BF16)
        gate = jnp.concatenate([dot(gates[block, t], pick, TN, HIGH) for t in (0, 1)], axis=0)
        gate = jnp.concatenate([gate, gate], axis=1)

        @pl.loop(0, 4)
        def _(i):
            part = down_tile(1 - c, i) * gate
            sibout[n, :, :, pl.ds(pl.multiple_of(i * 256, 256), 256)] = part.astype(BF16).reshape(2, T, 256)

        cross(n).start()

        @pl.loop(0, 4)
        def _(i):
            part = down_tile(c, i) * gate
            own[:, :, pl.ds(pl.multiple_of(i * 256, 256), 256)] = part.reshape(2, T, 256)

        cross(n).wait_recv()
        way = 0 if off >= 0 else 1
        for t in (0, 1):
            total = own[t] + sibin[n, t].astype(F32)
            if off == 4:
                ringout[t, 3, t] = total.astype(BF16)
                hop(t, 3, t).start()
                started.append((t, 3, t))
                continue
            j = abs(off)
            for came in (0, 1) if off == 0 else (way,):
                if j == 3 and came != t:
                    continue
                hop(came, j, t).wait_recv()
                total = total + ringin[came, j, t].astype(F32)
            if off:
                ringout[way, j - 1, t] = total.astype(BF16)
                hop(way, j - 1, t).start()
                started.append((way, j - 1, t))
            else:
                own[t] = total

    finout[...] = own[1 - c].astype(BF16)
    final = remote(finout, finin, fs.at[0], fr.at[0], sibling)
    final.start()
    here = pl.ds(pl.multiple_of(c * HALF, HALF), HALF)
    there = pl.ds(pl.multiple_of((1 - c) * HALF, HALF), HALF)
    out[:, here] = (mixed[:, here].astype(F32) + own[c]).astype(BF16)
    final.wait()
    out[:, there] = (mixed[:, there].astype(F32) + finin[...].astype(F32)).astype(BF16)

    for way, j, t in started:
        hop(way, j, t).wait_send()
    for n in range(8):
        cross(n).wait_send()
    for one in (tokens, gate_ring, up_z, up_x, down_z):
        one.sent()
    for o in range(1, NZ):
        to = ring(z, o, NZ)
        remote(mine.at[o], parts.at[z], z1s.at[o], z1r.at[o], on_z(to)).wait_send()
        remote(back.at[to], prior.at[z], z2s.at[o], z2r.at[o], on_z(to)).wait_send()
    for o in range(1, NX):
        remote(totals.at[x], totals.at[x], xs.at[o], xr.at[o], on_x(ring(x, o, NX))).wait_send()
        down_x(o, x).wait_send()


VMEM = pl.BlockSpec(memory_space=pltpu.VMEM)
ANY = pl.BlockSpec(memory_space=pl.ANY)
DMA = pltpu.SemaphoreType.DMA


def shards(q, k, v, res, s0, hg, fg, routes, route_gates, gate_w, up_w, down_w):
    experts = jnp.arange(EXPERTS, dtype=jnp.int32)[:, None]
    chosen, weight = routes[0].T, route_gates[0].T
    gt = jnp.zeros((EXPERTS, T), F32)
    for i in range(TOP):
        gt = gt + jnp.where(chosen[i][None] == experts, weight[i][None], 0.0)
    pieces = []
    for i in range(0, HID, HD):
        pieces += [gate_w[0][:, i : i + HD], up_w[0][:, i : i + HD]]
    gu = jnp.concatenate(pieces, axis=1)
    dt = jnp.pad(down_w[0].T, ((0, 0), (0, 768 - HID)))
    out = pl.pallas_call(
        kernel,
        out_shape=jax.ShapeDtypeStruct((T, D), BF16),
        in_specs=[ANY] * 7 + [VMEM] * 3,
        out_specs=VMEM,
        scratch_shapes=[
            pltpu.VMEM((T, D), BF16),
            pltpu.VMEM((T, D), BF16),
            pltpu.VMEM((T, D), BF16),
            pltpu.VMEM((T, D), BF16),
            pltpu.VMEM((HEADS, HD, HD), F32),
            pltpu.VMEM((NX, NZ, 64, 2 * HID), BF16),
            pltpu.VMEM((NX, NZ, 64, 768), BF16),
            pltpu.VMEM((NY, 2, 2, T, HALF), BF16),
            pltpu.VMEM((NY, 2, EXPERTS, T), F32),
            pltpu.VMEM((T, D), BF16),
            pltpu.VMEM((NZ, 2, HD, HD), BF16),
            pltpu.VMEM((NZ, 2, HD, HD), BF16),
            pltpu.VMEM((NZ, 2, HD, HD), BF16),
            pltpu.VMEM((NX, 2, HD, HD), BF16),
            pltpu.VMEM((NZ, 2, HD, HD), BF16),
            pltpu.VMEM((T, D), F32),
            pltpu.VMEM((2 * T, 768), BF16),
            pltpu.VMEM((2, T, HALF), F32),
            pltpu.VMEM((8, 2, T, HALF), BF16),
            pltpu.VMEM((8, 2, T, HALF), BF16),
            pltpu.VMEM((2, 4, 2, T, HALF), BF16),
            pltpu.VMEM((2, 4, 2, T, HALF), BF16),
            pltpu.VMEM((T, HALF), BF16),
            pltpu.VMEM((T, HALF), BF16),
            DMA((7,)),
            DMA((NZ,)), DMA((NZ,)), DMA((NX,)), DMA((NX,)), DMA((NZ,)), DMA((NZ,)),
            DMA((16,)), DMA((16,)), DMA((20,)), DMA((20,)),
            DMA((8,)), DMA((8,)), DMA((10,)), DMA((10,)),
            DMA((16,)), DMA((16,)), DMA((32,)), DMA((32,)),
            DMA((NX,)), DMA((NX,)), DMA((16,)), DMA((16,)),
            DMA((8,)), DMA((8,)), DMA((16,)), DMA((16,)), DMA((1,)), DMA((1,)),
        ],
        compiler_params=pltpu.CompilerParams(
            collective_id=0, has_side_effects=True, vmem_limit_bytes=56 * 2**20
        ),
        name="layer",
    )(q[0], k[0], v[0], res[0], s0[0], gu, dt, hg[None], fg[None], gt)
    return out[None]


def solution(mesh):
    placed = (
        P("ep", "seq", None),
        P("ep", "seq", None),
        P("ep", "seq", None),
        P("ep", "seq", None),
        P("ep", None, None, None),
        P(),
        P(),
        P("ep", "seq", None),
        P("ep", "seq", None),
        P("ep", "seq", None),
        P("ep", "seq", None),
        P("ep", None, "seq"),
    )
    return jax.shard_map(
        shards, mesh=mesh, in_specs=placed, out_specs=P("ep", "seq", None), check_vma=False
    )
```

```python
import functools

import jax
import jax.numpy as jnp
from jax import lax
from jax.experimental import pallas as pl
from jax.experimental.pallas import tpu as pltpu
from jax.sharding import PartitionSpec as P

D = 2048
HALF = 1024
HEADS = 16
HD = 128
HID = 704
EXPERTS = 16
TOP = 6
T = 128
NX, NZ, NY = 4, 8, 8
MESH = pl.DeviceIdType.MESH
F32 = jnp.float32
BF16 = jnp.bfloat16
HIGH = lax.Precision.HIGHEST
TN = (((0,), (0,)), ((), ()))
NT = (((1,), (1,)), ((), ()))
NN = (((1,), (0,)), ((), ()))


def dot(a, b, dims=NN, precision=None):
    return lax.dot_general(a, b, dims, precision=precision, preferred_element_type=F32)


def place():
    seq, ep = lax.axis_index("seq"), lax.axis_index("ep")
    return seq // NZ, lax.rem(seq, NZ), ep // 2, lax.rem(ep, 2)


def ring(at, step, size):
    return lax.rem(at + step + size, size)


def remote(src, dst, send, recv, device):
    return pltpu.make_async_remote_copy(
        src_ref=src, dst_ref=dst, send_sem=send, recv_sem=recv, device_id=device, device_id_type=MESH
    )


def cols(h):
    return pl.ds(pl.multiple_of(h * HD, HD), HD)


class Ring:
    def __init__(self, at, n, device, units, send, recv):
        self.at, self.n, self.device, self.units = at, n, device, units
        self.send, self.recv, self.started = send, recv, []

    def block(self, way, k):
        return ring(self.at, -(1 - 2 * way) * k, self.n)

    def copy(self, way, w, k, block):
        ref = self.units[w](block)
        i = (way * len(self.units) + w) * (self.n // 2) + k - 1
        to = self.device(ring(self.at, 1 - 2 * way, self.n))
        return remote(ref, ref, self.send.at[i], self.recv.at[i], to)

    def ways(self, w, k):
        return (0, 1) if k < self.n // 2 else (w % 2,)

    def hop(self, way, w, k):
        self.copy(way, w, k, self.block(way, k - 1)).start()
        self.started.append((way, w, k))

    def start(self, w):
        for way in (0, 1):
            self.hop(way, w, 1)

    def step(self, w, k):
        for way in self.ways(w, k):
            self.copy(way, w, k, self.block(way, k)).wait_recv()
            if k < self.n // 2 and way in self.ways(w, k + 1):
                self.hop(way, w, k + 1)

    def sent(self):
        for way, w, k in self.started:
            self.copy(way, w, k, self.block(way, k - 1)).wait_send()


class PairRing(Ring):
    def __init__(self, at, n, device, units, send, recv, core, sibling, cross_send, cross_recv):
        self.mine = [functools.partial(unit, core=core) for unit in units]
        self.other = [functools.partial(unit, core=1 - core) for unit in units]
        super().__init__(at, n, device, self.mine, send, recv)
        self.sibling, self.cross_send, self.cross_recv = sibling, cross_send, cross_recv
        self.crossed = []

    def across(self, way, w, k, units):
        ref = units[w](self.block(way, k))
        i = (way * len(units) + w) * (self.n // 2 + 1) + k
        return remote(ref, ref, self.cross_send.at[i], self.cross_recv.at[i], self.sibling)

    def cross(self, way, w, k):
        self.across(way, w, k, self.mine).start()
        self.crossed.append((way, w, k))

    def start(self, w):
        super().start(w)
        self.cross(0, w, 0)

    def step(self, w, k):
        super().step(w, k)
        for way in self.ways(w, k):
            self.cross(way, w, k)

    def came_across(self, steps):
        for way, w, k in self.crossed:
            if k in steps:
                self.across(way, w, k, self.other).wait_recv()

    def sent(self):
        super().sent()
        for way, w, k in self.crossed:
            self.across(way, w, k, self.mine).wait_send()


NEAR = (0, 1, -1, 2, -2, 3, -3, 4)


def kernel(
    q_in, k_in, v_in, res_in, s0_in, gate_in, up_in, down_in, hg, fg, gt,
    out,
    q, k, v, res, s0, gu, dt, rows, gates, mixed,
    mine, parts, back, totals, prior, base,
    gate_col, hidden, own, last, sibout, sibin, ringout, ringin, finout, finin,
    load, z1s, z1r, xs, xr, z2s, z2r, ys, yr, ycs, ycr, gs, gr, gcs, gcr,
    gzs, gzr, gxs, gxr, dxs, dxr, dzs, dzr, ss, sr, rs, rr, fs, fr,
):
    x, z, y, c = place()
    seq, ep = x * NZ + z, y * 2 + c
    per = HEADS // NZ
    sibling = (seq, y * 2 + 1 - c)
    loads = [
        pltpu.make_async_copy(src, dst, load.at[i])
        for i, (src, dst) in enumerate(
            [(k_in, k), (v_in, v), (q_in, q), (s0_in, s0), (res_in, res)]
        )
    ]
    for one in loads:
        one.start()
    near = (
        [(x * NZ + ring(z, o, NZ), ep) for o in range(1, NZ)]
        + [(ring(x, o, NX) * NZ + z, ep) for o in range(1, NX)]
        + [(seq, ring(y, o, NY) * 2 + c) for o in (1, -1)]
        + [sibling]
    )
    barrier = pltpu.get_barrier_semaphore()
    for device in near:
        pl.semaphore_signal(barrier, inc=1, device_id=device, device_id_type=MESH)
    for i in range(5):
        here = slice(i * HD, (i + 1) * HD)
        gu[x, z, :, i * 256 : i * 256 + HD] = gate_in[:, here]
        gu[x, z, :, i * 256 + HD : (i + 1) * 256] = up_in[:, here]
    gu[x, z, :, 1280:] = jnp.concatenate([gate_in[:, 640:], up_in[:, 640:]], axis=1)
    dt[x, z] = jnp.concatenate([down_in[...], jnp.zeros((64, 768 - HID), BF16)], axis=1)
    gates[y, c] = gt[...]
    pl.semaphore_wait(barrier, len(near))

    def on_x(place):
        return place * NZ + z, ep

    def on_y(place):
        return seq, place * 2 + c

    def on_z(place):
        return x * NZ + place, ep

    tokens = PairRing(
        y, NY, on_y, [lambda b, core, w=w: rows.at[b, core, w] for w in (0, 1)], ys, yr, c, sibling, ycs, ycr
    )
    gate_ring = PairRing(y, NY, on_y, [lambda b, core: gates.at[b, core]], gs, gr, c, sibling, gcs, gcr)
    up_z = Ring(z, NZ, on_z, [lambda b, w=w: gu.at[x, b, pl.ds(w * 32, 32)] for w in (0, 1)], gzs, gzr)
    up_x = Ring(x, NX, on_x, [lambda b, o=o: gu.at[b, ring(z, o, NZ)] for o in NEAR], gxs, gxr)
    down_z = Ring(z, NZ, on_z, [lambda b, w=w: dt.at[pl.ds(w * 2, 2), b] for w in (0, 1)], dzs, dzr)

    def down_x(o, frm):
        ref = dt.at[frm, z]
        return remote(ref, ref, dxs.at[o], dxr.at[o], on_x(ring(x, o, NX)))

    gate_ring.start(0)

    loads[0].wait()
    loads[1].wait()
    for o in list(range(1, NZ)) + [0]:
        owner = ring(z, o, NZ)
        for i in range(per):
            at_cols = cols(owner * per + i)
            state = dot(k[:, at_cols], v[:, at_cols], TN).astype(BF16)
            if o:
                mine[o, i] = state
            else:
                parts[z, i] = state
        if o:
            remote(mine.at[o], parts.at[z], z1s.at[o], z1r.at[o], on_z(owner)).start()
    for w in (0, 1):
        up_z.start(w)
    up_x.start(0)
    for o in range(1, NX):
        down_x(o, x).start()

    causal = lax.broadcasted_iota(jnp.int32, (T, T), 0) >= lax.broadcasted_iota(jnp.int32, (T, T), 1)
    loads[2].wait()
    loads[3].wait()

    @pl.loop(0, HEADS)
    def _(h):
        at_cols = cols(h)
        qh, kh = q[:, at_cols], k[:, at_cols]
        scores = jnp.where(causal, dot(qh, kh, NT), 0.0).astype(BF16)
        base[:, at_cols] = dot(scores, v[:, at_cols]) + dot(qh.astype(F32), s0[h], precision=HIGH)

    def up_step(n):
        for w in (0, 1):
            up_z.step(w, n)
        for w, o in enumerate(NEAR):
            if abs(o) == n:
                up_x.start(w)

    gate_ring.step(0, 1)
    for o in range(1, NZ):
        frm = ring(z, -o, NZ)
        remote(mine.at[o], parts.at[frm], z1s.at[o], z1r.at[o], on_z(frm)).wait_recv()
    total = jnp.zeros((per, HD, HD), F32)
    for o in range(NZ):
        total = total + parts[o].astype(F32)
    totals[x] = total.astype(BF16)
    for o in range(1, NX):
        remote(totals.at[x], totals.at[x], xs.at[o], xr.at[o], on_x(ring(x, o, NX))).start()
    up_step(1)
    gate_ring.step(0, 2)
    for o in range(1, NX):
        frm = ring(x, -o, NX)
        remote(totals.at[frm], totals.at[frm], xs.at[o], xr.at[o], on_x(frm)).wait_recv()
    state = jnp.zeros((per, HD, HD), F32)
    for o in range(NX - 1):
        state = state + jnp.where(o < x, totals[o].astype(F32), 0.0)
    for o in range(NZ):
        back[o] = state.astype(BF16)
        state = state + parts[o].astype(F32)
    for o in range(1, NZ):
        to = ring(z, o, NZ)
        remote(back.at[to], prior.at[z], z2s.at[o], z2r.at[o], on_z(to)).start()
    prior[z] = back[z]
    up_step(2)
    gate_ring.step(0, 3)
    up_x.step(0, 1)
    for o in range(1, NX):
        down_x(o, ring(x, -o, NX)).wait_recv()
    loads[4].wait()

    squares = jnp.zeros((T, 1), F32)
    for o in range(NZ):
        owner = ring(z, -o, NZ)
        if o:
            remote(back.at[owner], prior.at[owner], z2s.at[o], z2r.at[o], on_z(owner)).wait_recv()
        for i in range(per):
            at_cols = cols(owner * per + i)
            attended = base[:, at_cols] + dot(q[:, at_cols], prior[owner, i])
            scale = lax.rsqrt(jnp.mean(attended * attended, axis=-1, keepdims=True) + 1e-05)
            normed = attended * scale * hg[:, at_cols]
            row = (res[:, at_cols].astype(F32) + normed).astype(BF16)
            mixed[:, at_cols] = row
            wide = row.astype(F32)
            squares = squares + jnp.sum(wide * wide, axis=-1, keepdims=True)
    row_scale = lax.rsqrt(squares / D + 1e-05)
    for w in (0, 1):
        half = slice(w * HALF, (w + 1) * HALF)
        rows[y, c, w] = (mixed[:, half].astype(F32) * row_scale * fg[:, half]).astype(BF16)
        tokens.start(w)
    up_step(3)
    for w in (0, 1):
        down_z.start(w)
    gate_ring.step(0, 4)
    up_step(4)
    for n in range(1, 4):
        for w in (0, 1):
            tokens.step(w, n)
            if n == 1:
                up_x.step(w + 1, 1)
                down_z.step(w, 1)
            else:
                if 2 * n + w - 1 < len(NEAR):
                    up_x.step(2 * n + w - 1, 1)
                up_x.step(2 * n + w - 4, 2)
                down_z.step(w, n)
    gate_ring.came_across(range(5))
    pick = (lax.broadcasted_iota(jnp.int32, (EXPERTS, HD), 0) == ep).astype(F32)

    @pl.loop(0, NY)
    def _(b):
        for t in (0, 1):
            gate_col[b, t] = dot(gates[b, t], pick, TN, HIGH)

    low = lax.broadcasted_iota(jnp.int32, (1, HD), 1) < HID % HD

    def silu(gate_sum, up_sum):
        return gate_sum / (1.0 + jnp.exp(-gate_sum)) * up_sum

    def stack(parts):
        return parts[0] if len(parts) == 1 else jnp.concatenate(parts, axis=0)

    def expert_in(offs):
        blocks = [ring(y, off, NY) for off in offs]
        left, right = (stack([rows[b, :, u].reshape(2 * T, HALF) for b in blocks]) for u in (0, 1))

        def up_tile(tile):
            top = gu[0:2, :, :, tile].reshape(HALF, -1)
            bottom = gu[2:4, :, :, tile].reshape(HALF, -1)
            return dot(left, top) + dot(right, bottom)

        def keep(i, value):
            for n, off in enumerate(offs):
                hidden[off % NY, :, i * HD : (i + 1) * HD] = value[n * 2 * T : (n + 1) * 2 * T].astype(BF16)

        for i in range(5):
            both = up_tile(slice(i * 256, (i + 1) * 256))
            keep(i, silu(both[:, :HD], both[:, HD:]))
        both = up_tile(slice(1280, 1408))
        keep(5, jnp.where(low, silu(both, pltpu.roll(both, HD // 2, 1)), 0.0))

    def hop(way, j, t):
        n = (way * 4 + j) * 2 + t
        to = on_y(ring(y, 1 - 2 * way, NY))
        return remote(ringout.at[way, j, t], ringin.at[way, j, t], rs.at[n], rr.at[n], to)

    def cross(off):
        n = off % NY
        return remote(sibout.at[n], sibin.at[n], ss.at[n], sr.at[n], sibling)

    def expert_out(offs, keep):
        blocks = [ring(y, off, NY) for off in offs]
        rows_in = stack([hidden[off % NY] for off in offs])
        gate = stack([gate_col[b].reshape(2 * T, HD) for b in blocks])
        gate = jnp.concatenate([gate, gate], axis=1)

        def down_tile(half, i):
            piece = dt[half * 2 + i // 2, (i % 2) * 4 : (i % 2) * 4 + 4]
            return dot(rows_in, piece.reshape(256, 768), NT) * gate

        for i in range(4):
            part = down_tile(1 - c, i).astype(BF16)
            for n, off in enumerate(offs):
                sibout[off % NY, :, :, i * 256 : (i + 1) * 256] = part[n * 2 * T : (n + 1) * 2 * T].reshape(2, T, 256)
        for off in offs:
            cross(off).start()
        for i in range(4):
            part = down_tile(c, i)
            for n in range(len(offs)):
                keep[n, :, :, i * 256 : (i + 1) * 256] = part[n * 2 * T : (n + 1) * 2 * T].reshape(2, T, 256)

    started = []

    def send(way, j, t, total):
        ringout[way, j, t] = total.astype(BF16)
        hop(way, j, t).start()
        started.append((way, j, t))

    def pass_on(j, turn):
        for way in (0, 1):
            t = turn ^ 1 ^ way
            total = own[j - 1, way, t] + sibin[(j, NY - j)[way], t].astype(F32)
            if j < 3 or turn:
                hop(way, j, t).wait_recv()
                total = total + ringin[way, j, t].astype(F32)
            send(way, j - 1, t, total)

    up_x.step(7, 1)
    for n in (4, 5, 6, 7):
        up_x.step(n, 2)
    tokens.came_across((0, 1, 2, 3))
    expert_in((3, -3))
    tokens.step(0, 4)
    tokens.step(1, 4)
    down_z.step(0, 4)
    down_z.step(1, 4)
    expert_out((3, -3), own.at[2])
    for off in (3, -3):
        cross(off).wait_recv()
    pass_on(3, 0)
    tokens.came_across((4,))
    expert_in((4,))
    expert_out((4,), last)
    cross(4).wait_recv()
    for t in (0, 1):
        send(t, 3, t, last[0, t] + sibin[4, t].astype(F32))
    expert_in((2, -2))
    expert_out((2, -2), own.at[1])
    for off in (2, -2):
        cross(off).wait_recv()
    pass_on(2, 0)
    pass_on(3, 1)
    expert_in((1, -1))
    expert_out((1, -1), own.at[0])
    for off in (1, -1):
        cross(off).wait_recv()
    pass_on(1, 0)
    pass_on(2, 1)
    expert_in((0,))
    expert_out((0,), last)
    pass_on(1, 1)
    cross(0).wait_recv()
    for way in (0, 1):
        t = 1 - way
        hop(way, 0, t).wait_recv()
        last[0, t] = last[0, t] + sibin[0, t].astype(F32) + ringin[way, 0, t].astype(F32)

    def finish(t):
        return last[0, t] + ringin[t, 0, t].astype(F32)

    for way in (0, 1):
        hop(way, 0, way).wait_recv()
    finout[...] = finish(1 - c).astype(BF16)
    final = remote(finout, finin, fs.at[0], fr.at[0], sibling)
    final.start()
    here = pl.ds(pl.multiple_of(c * HALF, HALF), HALF)
    there = pl.ds(pl.multiple_of((1 - c) * HALF, HALF), HALF)
    out[:, here] = (mixed[:, here].astype(F32) + finish(c)).astype(BF16)
    final.wait()
    out[:, there] = (mixed[:, there].astype(F32) + finin[...].astype(F32)).astype(BF16)

    for way, j, t in started:
        hop(way, j, t).wait_send()
    for off in NEAR:
        cross(off).wait_send()
    for one in (tokens, gate_ring, up_z, up_x, down_z):
        one.sent()
    for o in range(1, NZ):
        to = ring(z, o, NZ)
        remote(mine.at[o], parts.at[z], z1s.at[o], z1r.at[o], on_z(to)).wait_send()
        remote(back.at[to], prior.at[z], z2s.at[o], z2r.at[o], on_z(to)).wait_send()
    for o in range(1, NX):
        remote(totals.at[x], totals.at[x], xs.at[o], xr.at[o], on_x(ring(x, o, NX))).wait_send()
        down_x(o, x).wait_send()


VMEM = pl.BlockSpec(memory_space=pltpu.VMEM)
ANY = pl.BlockSpec(memory_space=pl.ANY)
DMA = pltpu.SemaphoreType.DMA


def shards(q, k, v, res, s0, hg, fg, routes, route_gates, gate_w, up_w, down_w):
    experts = jnp.arange(EXPERTS, dtype=jnp.int32)[:, None]
    chosen, weight = routes[0].T, route_gates[0].T
    gt = jnp.zeros((EXPERTS, T), F32)
    for i in range(TOP):
        gt = gt + jnp.where(chosen[i][None] == experts, weight[i][None], 0.0)
    out = pl.pallas_call(
        kernel,
        out_shape=jax.ShapeDtypeStruct((T, D), BF16),
        in_specs=[ANY] * 5 + [VMEM] * 6,
        out_specs=VMEM,
        scratch_shapes=[
            pltpu.VMEM((T, D), BF16),
            pltpu.VMEM((T, D), BF16),
            pltpu.VMEM((T, D), BF16),
            pltpu.VMEM((T, D), BF16),
            pltpu.VMEM((HEADS, HD, HD), F32),
            pltpu.VMEM((NX, NZ, 64, 2 * HID), BF16),
            pltpu.VMEM((NX, NZ, 64, 768), BF16),
            pltpu.VMEM((NY, 2, 2, T, HALF), BF16),
            pltpu.VMEM((NY, 2, EXPERTS, T), F32),
            pltpu.VMEM((T, D), BF16),
            pltpu.VMEM((NZ, 2, HD, HD), BF16),
            pltpu.VMEM((NZ, 2, HD, HD), BF16),
            pltpu.VMEM((NZ, 2, HD, HD), BF16),
            pltpu.VMEM((NX, 2, HD, HD), BF16),
            pltpu.VMEM((NZ, 2, HD, HD), BF16),
            pltpu.VMEM((T, D), F32),
            pltpu.VMEM((NY, 2, T, HD), F32),
            pltpu.VMEM((NY, 2 * T, 768), BF16),
            pltpu.VMEM((3, 2, 2, T, HALF), F32),
            pltpu.VMEM((1, 2, T, HALF), F32),
            pltpu.VMEM((8, 2, T, HALF), BF16),
            pltpu.VMEM((8, 2, T, HALF), BF16),
            pltpu.VMEM((2, 4, 2, T, HALF), BF16),
            pltpu.VMEM((2, 4, 2, T, HALF), BF16),
            pltpu.VMEM((T, HALF), BF16),
            pltpu.VMEM((T, HALF), BF16),
            DMA((5,)),
            DMA((NZ,)), DMA((NZ,)), DMA((NX,)), DMA((NX,)), DMA((NZ,)), DMA((NZ,)),
            DMA((16,)), DMA((16,)), DMA((20,)), DMA((20,)),
            DMA((8,)), DMA((8,)), DMA((10,)), DMA((10,)),
            DMA((16,)), DMA((16,)), DMA((32,)), DMA((32,)),
            DMA((NX,)), DMA((NX,)), DMA((16,)), DMA((16,)),
            DMA((8,)), DMA((8,)), DMA((16,)), DMA((16,)), DMA((1,)), DMA((1,)),
        ],
        compiler_params=pltpu.CompilerParams(
            collective_id=0, has_side_effects=True, vmem_limit_bytes=56 * 2**20
        ),
        name="layer",
    )(q[0], k[0], v[0], res[0], s0[0], gate_w[0], up_w[0], down_w[0].T, hg[None], fg[None], gt)
    return out[None]


def solution(mesh):
    placed = (
        P("ep", "seq", None),
        P("ep", "seq", None),
        P("ep", "seq", None),
        P("ep", "seq", None),
        P("ep", None, None, None),
        P(),
        P(),
        P("ep", "seq", None),
        P("ep", "seq", None),
        P("ep", "seq", None),
        P("ep", "seq", None),
        P("ep", None, "seq"),
    )
    return jax.shard_map(
        shards, mesh=mesh, in_specs=placed, out_specs=P("ep", "seq", None), check_vma=False
    )
```

```python
import functools

import jax
import jax.numpy as jnp
from jax import lax
from jax.experimental import pallas as pl
from jax.experimental.pallas import tpu as pltpu
from jax.sharding import PartitionSpec as P

D = 2048
HALF = 1024
HEADS = 16
HD = 128
HID = 704
EXPERTS = 16
TOP = 6
T = 128
NX, NZ, NY = 4, 8, 8
MESH = pl.DeviceIdType.MESH
F32 = jnp.float32
BF16 = jnp.bfloat16
HIGH = lax.Precision.HIGHEST
TN = (((0,), (0,)), ((), ()))
NT = (((1,), (1,)), ((), ()))
NN = (((1,), (0,)), ((), ()))


def dot(a, b, dims=NN, precision=None):
    return lax.dot_general(a, b, dims, precision=precision, preferred_element_type=F32)


def place():
    seq, ep = lax.axis_index("seq"), lax.axis_index("ep")
    return seq // NZ, lax.rem(seq, NZ), ep // 2, lax.rem(ep, 2)


def ring(at, step, size):
    return lax.rem(at + step + size, size)


def remote(src, dst, send, recv, device):
    return pltpu.make_async_remote_copy(
        src_ref=src, dst_ref=dst, send_sem=send, recv_sem=recv, device_id=device, device_id_type=MESH
    )


def cols(h):
    return pl.ds(pl.multiple_of(h * HD, HD), HD)


class Ring:
    def __init__(self, at, n, device, units, send, recv):
        self.at, self.n, self.device, self.units = at, n, device, units
        self.send, self.recv, self.started = send, recv, []

    def block(self, way, k):
        return ring(self.at, -(1 - 2 * way) * k, self.n)

    def copy(self, way, w, k, block):
        ref = self.units[w](block)
        i = (way * len(self.units) + w) * (self.n // 2) + k - 1
        to = self.device(ring(self.at, 1 - 2 * way, self.n))
        return remote(ref, ref, self.send.at[i], self.recv.at[i], to)

    def ways(self, w, k):
        return (0, 1) if k < self.n // 2 else (w % 2,)

    def hop(self, way, w, k):
        self.copy(way, w, k, self.block(way, k - 1)).start()
        self.started.append((way, w, k))

    def start(self, w):
        for way in (0, 1):
            self.hop(way, w, 1)

    def step(self, w, k):
        for way in self.ways(w, k):
            self.copy(way, w, k, self.block(way, k)).wait_recv()
            if k < self.n // 2 and way in self.ways(w, k + 1):
                self.hop(way, w, k + 1)

    def sent(self):
        for way, w, k in self.started:
            self.copy(way, w, k, self.block(way, k - 1)).wait_send()


class PairRing(Ring):
    def __init__(self, at, n, device, units, send, recv, core, sibling, cross_send, cross_recv):
        self.mine = [functools.partial(unit, core=core) for unit in units]
        self.other = [functools.partial(unit, core=1 - core) for unit in units]
        super().__init__(at, n, device, self.mine, send, recv)
        self.sibling, self.cross_send, self.cross_recv = sibling, cross_send, cross_recv
        self.crossed = []

    def across(self, way, w, k, units):
        ref = units[w](self.block(way, k))
        i = (way * len(units) + w) * (self.n // 2 + 1) + k
        return remote(ref, ref, self.cross_send.at[i], self.cross_recv.at[i], self.sibling)

    def cross(self, way, w, k):
        self.across(way, w, k, self.mine).start()
        self.crossed.append((way, w, k))

    def start(self, w):
        super().start(w)
        self.cross(0, w, 0)

    def step(self, w, k):
        super().step(w, k)
        for way in self.ways(w, k):
            self.cross(way, w, k)

    def came_across(self, steps):
        for way, w, k in self.crossed:
            if k in steps:
                self.across(way, w, k, self.other).wait_recv()

    def sent(self):
        super().sent()
        for way, w, k in self.crossed:
            self.across(way, w, k, self.mine).wait_send()


NEAR = (0, 1, -1, 2, -2, 3, -3, 4)


def kernel(
    q_in, k_in, v_in, res_in, s0_in, gate_in, up_in, down_in, hg, fg, gt,
    out,
    q, k, v, res, s0, gu, dt, rows, gates, mixed,
    mine, parts, back, totals, prior, base,
    gate_col, hidden, own, last, sibout, sibin, ringout, ringin, finout, finin,
    load, z1s, z1r, xs, xr, z2s, z2r, ys, yr, ycs, ycr, gs, gr, gcs, gcr,
    gzs, gzr, gxs, gxr, dxs, dxr, dzs, dzr, ss, sr, rs, rr, fs, fr,
):
    x, z, y, c = place()
    seq, ep = x * NZ + z, y * 2 + c
    per = HEADS // NZ
    sibling = (seq, y * 2 + 1 - c)
    loads = [
        pltpu.make_async_copy(src, dst, load.at[i])
        for i, (src, dst) in enumerate(
            [(k_in, k), (v_in, v), (q_in, q), (s0_in, s0), (res_in, res)]
        )
    ]
    for one in loads:
        one.start()
    near = (
        [(x * NZ + ring(z, o, NZ), ep) for o in range(1, NZ)]
        + [(ring(x, o, NX) * NZ + z, ep) for o in range(1, NX)]
        + [(seq, ring(y, o, NY) * 2 + c) for o in (1, -1)]
        + [sibling]
    )
    barrier = pltpu.get_barrier_semaphore()
    for device in near:
        pl.semaphore_signal(barrier, inc=1, device_id=device, device_id_type=MESH)
    for i in range(5):
        here = slice(i * HD, (i + 1) * HD)
        gu[x, z, :, i * 256 : i * 256 + HD] = gate_in[:, here]
        gu[x, z, :, i * 256 + HD : (i + 1) * 256] = up_in[:, here]
    gu[x, z, :, 1280:] = jnp.concatenate([gate_in[:, 640:], up_in[:, 640:]], axis=1)
    dt[x, z] = jnp.concatenate([down_in[...], jnp.zeros((64, 768 - HID), BF16)], axis=1)
    gates[y, c] = gt[...]
    loads[0].wait()
    loads[1].wait()
    for o in range(NZ):
        for i in range(per):
            at_cols = cols(ring(z, o, NZ) * per + i)
            state = dot(k[:, at_cols], v[:, at_cols], TN).astype(BF16)
            if o:
                mine[o, i] = state
            else:
                parts[z, i] = state
    pl.semaphore_wait(barrier, len(near))

    def on_x(place):
        return place * NZ + z, ep

    def on_y(place):
        return seq, place * 2 + c

    def on_z(place):
        return x * NZ + place, ep

    tokens = PairRing(
        y, NY, on_y, [lambda b, core, w=w: rows.at[b, core, w] for w in (0, 1)], ys, yr, c, sibling, ycs, ycr
    )
    gate_ring = PairRing(y, NY, on_y, [lambda b, core: gates.at[b, core]], gs, gr, c, sibling, gcs, gcr)
    up_z = Ring(z, NZ, on_z, [lambda b, w=w: gu.at[x, b, pl.ds(w * 32, 32)] for w in (0, 1)], gzs, gzr)
    up_x = Ring(x, NX, on_x, [lambda b, o=o: gu.at[b, ring(z, o, NZ)] for o in NEAR], gxs, gxr)
    down_z = Ring(z, NZ, on_z, [lambda b, w=w: dt.at[pl.ds(w * 2, 2), b] for w in (0, 1)], dzs, dzr)

    def down_x(o, frm):
        ref = dt.at[frm, z]
        return remote(ref, ref, dxs.at[o], dxr.at[o], on_x(ring(x, o, NX)))

    gate_ring.start(0)

    for o in range(1, NZ):
        remote(mine.at[o], parts.at[z], z1s.at[o], z1r.at[o], on_z(ring(z, o, NZ))).start()
    for w in (0, 1):
        up_z.start(w)
    up_x.start(0)
    for o in range(1, NX):
        down_x(o, x).start()

    causal = lax.broadcasted_iota(jnp.int32, (T, T), 0) >= lax.broadcasted_iota(jnp.int32, (T, T), 1)
    loads[2].wait()
    loads[3].wait()

    @pl.loop(0, HEADS)
    def _(h):
        at_cols = cols(h)
        qh, kh = q[:, at_cols], k[:, at_cols]
        scores = jnp.where(causal, dot(qh, kh, NT), 0.0).astype(BF16)
        base[:, at_cols] = dot(scores, v[:, at_cols]) + dot(qh.astype(F32), s0[h], precision=HIGH)

    def up_step(n):
        for w in (0, 1):
            up_z.step(w, n)
        for w, o in enumerate(NEAR):
            if abs(o) == n:
                up_x.start(w)

    gate_ring.step(0, 1)
    for o in range(1, NZ):
        frm = ring(z, -o, NZ)
        remote(mine.at[o], parts.at[frm], z1s.at[o], z1r.at[o], on_z(frm)).wait_recv()
    total = jnp.zeros((per, HD, HD), F32)
    for o in range(NZ):
        total = total + parts[o].astype(F32)
    totals[x] = total.astype(BF16)
    for o in range(1, NX):
        remote(totals.at[x], totals.at[x], xs.at[o], xr.at[o], on_x(ring(x, o, NX))).start()
    up_step(1)
    gate_ring.step(0, 2)
    for o in range(1, NX):
        frm = ring(x, -o, NX)
        remote(totals.at[frm], totals.at[frm], xs.at[o], xr.at[o], on_x(frm)).wait_recv()
    state = jnp.zeros((per, HD, HD), F32)
    for o in range(NX - 1):
        state = state + jnp.where(o < x, totals[o].astype(F32), 0.0)
    for o in range(NZ):
        back[o] = state.astype(BF16)
        state = state + parts[o].astype(F32)
    for o in range(1, NZ):
        to = ring(z, o, NZ)
        remote(back.at[to], prior.at[z], z2s.at[o], z2r.at[o], on_z(to)).start()
    prior[z] = back[z]
    loads[4].wait()

    squares = jnp.zeros((T, 1), F32)
    for o in range(NZ):
        owner = ring(z, -o, NZ)
        if o:
            remote(back.at[owner], prior.at[owner], z2s.at[o], z2r.at[o], on_z(owner)).wait_recv()
        if o == 2:
            up_step(2)
        for i in range(per):
            at_cols = cols(owner * per + i)
            attended = base[:, at_cols] + dot(q[:, at_cols], prior[owner, i])
            scale = lax.rsqrt(jnp.mean(attended * attended, axis=-1, keepdims=True) + 1e-05)
            normed = attended * scale * hg[:, at_cols]
            row = (res[:, at_cols].astype(F32) + normed).astype(BF16)
            mixed[:, at_cols] = row
            wide = row.astype(F32)
            squares = squares + jnp.sum(wide * wide, axis=-1, keepdims=True)
    row_scale = lax.rsqrt(squares / D + 1e-05)
    for w in (0, 1):
        half = slice(w * HALF, (w + 1) * HALF)
        rows[y, c, w] = (mixed[:, half].astype(F32) * row_scale * fg[:, half]).astype(BF16)
        tokens.start(w)
    gate_ring.step(0, 3)
    for o in range(1, NX):
        down_x(o, ring(x, -o, NX)).wait_recv()
    for w in (0, 1):
        down_z.start(w)
    up_step(3)
    up_x.step(0, 1)
    for n in range(1, 4):
        for w in (0, 1):
            tokens.step(w, n)
            if n == 1 and w == 0:
                up_step(4)
                gate_ring.step(0, 4)
            if n == 1:
                up_x.step(w + 1, 1)
                down_z.step(w, 1)
            else:
                if 2 * n + w - 1 < len(NEAR):
                    up_x.step(2 * n + w - 1, 1)
                up_x.step(2 * n + w - 4, 2)
                down_z.step(w, n)
    gate_ring.came_across(range(5))
    pick = (lax.broadcasted_iota(jnp.int32, (EXPERTS, HD), 0) == ep).astype(F32)

    @pl.loop(0, NY)
    def _(b):
        for t in (0, 1):
            gate_col[b, t] = dot(gates[b, t], pick, TN, HIGH)

    low = lax.broadcasted_iota(jnp.int32, (1, HD), 1) < HID % HD

    def silu(gate_sum, up_sum):
        return gate_sum / (1.0 + jnp.exp(-gate_sum)) * up_sum

    def stack(parts):
        return parts[0] if len(parts) == 1 else jnp.concatenate(parts, axis=0)

    def expert_in(offs):
        blocks = [ring(y, off, NY) for off in offs]
        left, right = (stack([rows[b, :, u].reshape(2 * T, HALF) for b in blocks]) for u in (0, 1))

        def up_tile(tile):
            top = gu[0:2, :, :, tile].reshape(HALF, -1)
            bottom = gu[2:4, :, :, tile].reshape(HALF, -1)
            return dot(left, top) + dot(right, bottom)

        def keep(i, value):
            for n, off in enumerate(offs):
                hidden[off % NY, :, i * HD : (i + 1) * HD] = value[n * 2 * T : (n + 1) * 2 * T].astype(BF16)

        for i in range(5):
            both = up_tile(slice(i * 256, (i + 1) * 256))
            keep(i, silu(both[:, :HD], both[:, HD:]))
        both = up_tile(slice(1280, 1408))
        keep(5, jnp.where(low, silu(both, pltpu.roll(both, HD // 2, 1)), 0.0))

    def hop(way, j, t):
        n = (way * 4 + j) * 2 + t
        to = on_y(ring(y, 1 - 2 * way, NY))
        return remote(ringout.at[way, j, t], ringin.at[way, j, t], rs.at[n], rr.at[n], to)

    def cross(off):
        n = off % NY
        return remote(sibout.at[n], sibin.at[n], ss.at[n], sr.at[n], sibling)

    def expert_out(offs, keep):
        blocks = [ring(y, off, NY) for off in offs]
        rows_in = stack([hidden[off % NY] for off in offs])
        gate = stack([gate_col[b].reshape(2 * T, HD) for b in blocks])
        gate = jnp.concatenate([gate, gate], axis=1)

        def down_tile(half, i):
            piece = dt[half * 2 + i // 2, (i % 2) * 4 : (i % 2) * 4 + 4]
            return dot(rows_in, piece.reshape(256, 768), NT) * gate

        for i in range(4):
            part = down_tile(1 - c, i).astype(BF16)
            for n, off in enumerate(offs):
                sibout[off % NY, :, :, i * 256 : (i + 1) * 256] = part[n * 2 * T : (n + 1) * 2 * T].reshape(2, T, 256)
        for off in offs:
            cross(off).start()
        for i in range(4):
            part = down_tile(c, i)
            for n in range(len(offs)):
                keep[n, :, :, i * 256 : (i + 1) * 256] = part[n * 2 * T : (n + 1) * 2 * T].reshape(2, T, 256)

    started = []

    def send(way, j, t, total):
        ringout[way, j, t] = total.astype(BF16)
        hop(way, j, t).start()
        started.append((way, j, t))

    def pass_on(j, turn):
        for way in (0, 1):
            t = turn ^ 1 ^ way
            total = own[j - 1, way, t] + sibin[(j, NY - j)[way], t].astype(F32)
            if j < 3 or turn:
                hop(way, j, t).wait_recv()
                total = total + ringin[way, j, t].astype(F32)
            send(way, j - 1, t, total)

    up_x.step(7, 1)
    for n in (4, 5, 6, 7):
        up_x.step(n, 2)
    tokens.came_across((0, 1, 2, 3))
    expert_in((3, -3))
    tokens.step(0, 4)
    tokens.step(1, 4)
    down_z.step(0, 4)
    down_z.step(1, 4)
    expert_out((3, -3), own.at[2])
    for off in (3, -3):
        cross(off).wait_recv()
    pass_on(3, 0)
    tokens.came_across((4,))
    expert_in((4,))
    expert_out((4,), last)
    cross(4).wait_recv()
    for t in (0, 1):
        send(t, 3, t, last[0, t] + sibin[4, t].astype(F32))
    expert_in((2, -2))
    expert_out((2, -2), own.at[1])
    for off in (2, -2):
        cross(off).wait_recv()
    pass_on(2, 0)
    pass_on(3, 1)
    expert_in((1, -1))
    expert_out((1, -1), own.at[0])
    for off in (1, -1):
        cross(off).wait_recv()
    pass_on(1, 0)
    pass_on(2, 1)
    expert_in((0,))
    expert_out((0,), last)
    pass_on(1, 1)
    cross(0).wait_recv()
    for way in (0, 1):
        t = 1 - way
        hop(way, 0, t).wait_recv()
        last[0, t] = last[0, t] + sibin[0, t].astype(F32) + ringin[way, 0, t].astype(F32)

    def finish(t):
        return last[0, t] + ringin[t, 0, t].astype(F32)

    for way in (0, 1):
        hop(way, 0, way).wait_recv()
    finout[...] = finish(1 - c).astype(BF16)
    final = remote(finout, finin, fs.at[0], fr.at[0], sibling)
    final.start()
    here = pl.ds(pl.multiple_of(c * HALF, HALF), HALF)
    there = pl.ds(pl.multiple_of((1 - c) * HALF, HALF), HALF)
    out[:, here] = (mixed[:, here].astype(F32) + finish(c)).astype(BF16)
    final.wait()
    out[:, there] = (mixed[:, there].astype(F32) + finin[...].astype(F32)).astype(BF16)

    for way, j, t in started:
        hop(way, j, t).wait_send()
    for off in NEAR:
        cross(off).wait_send()
    for one in (tokens, gate_ring, up_z, up_x, down_z):
        one.sent()
    for o in range(1, NZ):
        to = ring(z, o, NZ)
        remote(mine.at[o], parts.at[z], z1s.at[o], z1r.at[o], on_z(to)).wait_send()
        remote(back.at[to], prior.at[z], z2s.at[o], z2r.at[o], on_z(to)).wait_send()
    for o in range(1, NX):
        remote(totals.at[x], totals.at[x], xs.at[o], xr.at[o], on_x(ring(x, o, NX))).wait_send()
        down_x(o, x).wait_send()


VMEM = pl.BlockSpec(memory_space=pltpu.VMEM)
ANY = pl.BlockSpec(memory_space=pl.ANY)
DMA = pltpu.SemaphoreType.DMA


def shards(q, k, v, res, s0, hg, fg, routes, route_gates, gate_w, up_w, down_w):
    experts = jnp.arange(EXPERTS, dtype=jnp.int32)[:, None]
    chosen, weight = routes[0].T, route_gates[0].T
    gt = jnp.zeros((EXPERTS, T), F32)
    for i in range(TOP):
        gt = gt + jnp.where(chosen[i][None] == experts, weight[i][None], 0.0)
    out = pl.pallas_call(
        kernel,
        out_shape=jax.ShapeDtypeStruct((T, D), BF16),
        in_specs=[ANY] * 5 + [VMEM] * 6,
        out_specs=VMEM,
        scratch_shapes=[
            pltpu.VMEM((T, D), BF16),
            pltpu.VMEM((T, D), BF16),
            pltpu.VMEM((T, D), BF16),
            pltpu.VMEM((T, D), BF16),
            pltpu.VMEM((HEADS, HD, HD), F32),
            pltpu.VMEM((NX, NZ, 64, 2 * HID), BF16),
            pltpu.VMEM((NX, NZ, 64, 768), BF16),
            pltpu.VMEM((NY, 2, 2, T, HALF), BF16),
            pltpu.VMEM((NY, 2, EXPERTS, T), F32),
            pltpu.VMEM((T, D), BF16),
            pltpu.VMEM((NZ, 2, HD, HD), BF16),
            pltpu.VMEM((NZ, 2, HD, HD), BF16),
            pltpu.VMEM((NZ, 2, HD, HD), BF16),
            pltpu.VMEM((NX, 2, HD, HD), BF16),
            pltpu.VMEM((NZ, 2, HD, HD), BF16),
            pltpu.VMEM((T, D), F32),
            pltpu.VMEM((NY, 2, T, HD), F32),
            pltpu.VMEM((NY, 2 * T, 768), BF16),
            pltpu.VMEM((3, 2, 2, T, HALF), F32),
            pltpu.VMEM((1, 2, T, HALF), F32),
            pltpu.VMEM((8, 2, T, HALF), BF16),
            pltpu.VMEM((8, 2, T, HALF), BF16),
            pltpu.VMEM((2, 4, 2, T, HALF), BF16),
            pltpu.VMEM((2, 4, 2, T, HALF), BF16),
            pltpu.VMEM((T, HALF), BF16),
            pltpu.VMEM((T, HALF), BF16),
            DMA((5,)),
            DMA((NZ,)), DMA((NZ,)), DMA((NX,)), DMA((NX,)), DMA((NZ,)), DMA((NZ,)),
            DMA((16,)), DMA((16,)), DMA((20,)), DMA((20,)),
            DMA((8,)), DMA((8,)), DMA((10,)), DMA((10,)),
            DMA((16,)), DMA((16,)), DMA((32,)), DMA((32,)),
            DMA((NX,)), DMA((NX,)), DMA((16,)), DMA((16,)),
            DMA((8,)), DMA((8,)), DMA((16,)), DMA((16,)), DMA((1,)), DMA((1,)),
        ],
        compiler_params=pltpu.CompilerParams(
            collective_id=0, has_side_effects=True, vmem_limit_bytes=56 * 2**20
        ),
        name="layer",
    )(q[0], k[0], v[0], res[0], s0[0], gate_w[0], up_w[0], down_w[0].T, hg[None], fg[None], gt)
    return out[None]


def solution(mesh):
    placed = (
        P("ep", "seq", None),
        P("ep", "seq", None),
        P("ep", "seq", None),
        P("ep", "seq", None),
        P("ep", None, None, None),
        P(),
        P(),
        P("ep", "seq", None),
        P("ep", "seq", None),
        P("ep", "seq", None),
        P("ep", "seq", None),
        P("ep", None, "seq"),
    )
    return jax.shard_map(
        shards, mesh=mesh, in_specs=placed, out_specs=P("ep", "seq", None), check_vma=False
    )
```
